32 devices in a mesh: gx: 8 (over z, y), gy: 4 (over x, core).
Axes of the slice: x: 2, y: 2, z: 4, core: 2. Of those that a mesh axis runs over, the one named last changes fastest.
Arguments:
- populations: float32 [27, 64, 8192], P(None, 'gx', 'gy'), may hold values from 0.6 to 1.4
- marker_site: int32 [4, 16384], P(None, ('gx', 'gy')), may hold values from 0 to 63, as said below
- marker_frac: float32 [3, 16384], P(None, ('gx', 'gy')), may hold values from 0 to 1
- marker_force: float32 [3, 16384], P(None, ('gx', 'gy')), may hold values from -2 to 2
- marker_count: int32 [8], P('gx'), may hold values from 256 to 2048, as said below
Outputs:
- populations_next: float32 [27, 64, 8192], P(None, 'gx', 'gy')
The draws below stay inside these ranges and needn't reach their ends.
Inputs may be any that keep to these rules, and one draw needn't show every extreme that they name: `marker_site`: row 0 is the owning tile's row, below 4; rows 1, 2, 3 are cell offsets inside that tile, below 8, 32 and 64. The owning tile lies in the column of the slot. A column's live markers fill its first marker_count slots; some column is full in every draw.
All inputs are finite; a program needn't handle non-finite values.
Results may differ from the reference program's by a relative error of at most 0.0003.
Values sent between devices are 32-bit elements; how exact they have to be, the bound alone decides.
A program may use at most 64 MiB of HBM per device.

```python
import jax
import jax.numpy as jnp
from jax import lax

CX = 8
CY = 32
NZ = 64
NX = 64
NY = 128
MCOL = 2048
MARKERS = 16384


def draw_marker_site(key, part):
    streams = jax.random.split(jax.random.fold_in(key, 11), 4)
    tile_row = jax.random.randint(streams[0], (MARKERS,), 0, NY // CY)
    offset_x = jax.random.randint(streams[1], (MARKERS,), 0, CX)
    offset_y = jax.random.randint(streams[2], (MARKERS,), 0, CY)
    offset_z = jax.random.randint(streams[3], (MARKERS,), 0, NZ)
    return jnp.stack([tile_row, offset_x, offset_y, offset_z], 0).astype(jnp.int32)


def draw_marker_count(key, part):
    streams = jax.random.split(jax.random.fold_in(key, 23), 2)
    columns = NX // CX
    counts = jax.random.randint(streams[0], (columns,), MCOL // 8, MCOL // 2 + 1)
    first_full = jax.random.randint(streams[1], (), 0, columns)
    second_full = (first_full + columns // 2) % columns
    counts = counts.at[first_full].set(MCOL).at[second_full].set(MCOL)
    return counts.astype(jnp.int32)


def shard_levels(own_key, extent, pieces, least, top_value):
    gain = 1.0
    for axis_at, blocks in pieces:
        heights = jax.random.uniform(jax.random.fold_in(jax.random.fold_in(own_key, 6), axis_at), (blocks,), jnp.float32, least / len(pieces), top_value / len(pieces))
        gain = gain * jnp.repeat(jnp.exp(heights), extent[axis_at] // blocks).reshape((-1,) + (1,) * (len(extent) - 1 - axis_at))
    return gain


def centred(stream_key, shape, scale, reach, pieces=(), kind=jnp.bfloat16):
    drawn = jax.random.normal(stream_key, shape, jnp.float32) * scale
    if len(pieces) > 0:
        drawn = shard_levels(stream_key, shape, pieces, -0.22, 0.18) * drawn
    return jnp.clip(drawn, min=-reach, max=reach).astype(kind)


def setup_inputs(seed: int = 0) -> dict:
    splits = jax.random.split(jax.random.key(seed), 6)
    return {
        "populations": jnp.clip(0.6 + 0.79999995 * jax.random.uniform(splits[0], (27, NX, NY * NZ), jnp.float32) ** shard_levels(splits[0], (27, NX, NY * NZ), ((1, 8), (2, 4)), -0.2, 0.2), 0.6, 1.4),
        "marker_site": draw_marker_site(jax.random.fold_in(splits[5], 71), 0),
        "marker_frac": jnp.clip(1.0 * jax.random.uniform(splits[2], (3, MARKERS), jnp.float32) ** shard_levels(splits[2], (3, MARKERS), ((1, 32),), -0.2, 0.2), 0.0, 1.0),
        "marker_force": centred(splits[3], (3, MARKERS), 0.3, 2.0, ((1, 32),), jnp.float32),
        "marker_count": draw_marker_count(jax.random.fold_in(splits[5], 71), 0),
    }


RELAX_RATE = 1.8
LINE_WEIGHTS = (1.0 / 6.0, 2.0 / 3.0, 1.0 / 6.0)


def gaussian_moment(labels, covariance):
    if len(labels) == 0:
        return None
    result = None
    for position in range(1, len(labels)):
        remaining = labels[1:position] + labels[position + 1:]
        lower_label = min(labels[0], labels[position])
        upper_label = max(labels[0], labels[position])
        product = covariance[(lower_label, upper_label)]
        inner = gaussian_moment(remaining, covariance)
        if inner is not None:
            product = product * inner
        result = product if result is None else result + product
    return result


def forward_line(lower_pop, centre_pop, upper_pop, velocity):
    summed = lower_pop + centre_pop + upper_pop
    first_order = upper_pop - lower_pop - velocity * summed
    second_order = (upper_pop * (1.0 - velocity) * (1.0 - velocity)
                    + lower_pop * (1.0 + velocity) * (1.0 + velocity)
                    + centre_pop * velocity * velocity)
    return summed, first_order, second_order


def backward_line(zeroth, first_order, second_order, velocity):
    square = velocity * velocity
    centre_pop = zeroth * (1.0 - square) - 2.0 * velocity * first_order - second_order
    lower_pop = 0.5 * (zeroth * (square - velocity) + first_order * (2.0 * velocity - 1.0) + second_order)
    upper_pop = 0.5 * (zeroth * (square + velocity) + first_order * (2.0 * velocity + 1.0) + second_order)
    return lower_pop, centre_pop, upper_pop


def place_slot(axis_pick, slot, outer, inner):
    if axis_pick == 0:
        return (slot, outer, inner)
    if axis_pick == 1:
        return (outer, slot, inner)
    return (outer, inner, slot)


def transform(grid, velocity, axis_pick, line_fn):
    result = dict(grid)
    for outer in range(3):
        for inner in range(3):
            triples = [place_slot(axis_pick, slot, outer, inner) for slot in range(3)]
            outputs = line_fn(grid[triples[0]], grid[triples[1]], grid[triples[2]], velocity)
            for slot in range(3):
                result[triples[slot]] = outputs[slot]
    return result


def collide(populations, force):
    grid = {}
    weights = []
    for index in range(27):
        triple = (index // 9, (index // 3) % 3, index % 3)
        weight = LINE_WEIGHTS[triple[0]] * LINE_WEIGHTS[triple[1]] * LINE_WEIGHTS[triple[2]]
        weights.append(weight)
        grid[triple] = weight * populations[index]
    density = sum(grid.values())
    velocity = []
    for axis_pick in range(3):
        momentum = sum(grid[triple] for triple in grid if triple[axis_pick] == 2) - sum(
            grid[triple] for triple in grid if triple[axis_pick] == 0)
        velocity.append((momentum + 0.5 * force[axis_pick]) / density)
    moments = transform(grid, velocity[2], 2, forward_line)
    moments = transform(moments, velocity[1], 1, forward_line)
    moments = transform(moments, velocity[0], 0, forward_line)
    second = {(0, 0): moments[(2, 0, 0)], (1, 1): moments[(0, 2, 0)], (2, 2): moments[(0, 0, 2)],
              (0, 1): moments[(1, 1, 0)], (0, 2): moments[(1, 0, 1)], (1, 2): moments[(0, 1, 1)]}
    trace_third = (second[(0, 0)] + second[(1, 1)] + second[(2, 2)]) / 3.0
    covariance = {}
    for entry_pair in second:
        if entry_pair[0] == entry_pair[1]:
            relaxed = density / 3.0 + (1.0 - RELAX_RATE) * (second[entry_pair] - trace_third)
        else:
            relaxed = (1.0 - RELAX_RATE) * second[entry_pair]
        covariance[entry_pair] = relaxed / density
    post_moments = {}
    for triple in moments:
        total_order = triple[0] + triple[1] + triple[2]
        labels = [0] * triple[0] + [1] * triple[1] + [2] * triple[2]
        if total_order == 0:
            post_moments[triple] = density
        elif total_order == 1:
            post_moments[triple] = 0.5 * force[labels[0]]
        elif total_order % 2 == 1:
            post_moments[triple] = jnp.zeros_like(density)
        else:
            post_moments[triple] = density * gaussian_moment(labels, covariance)
    restored = transform(post_moments, velocity[0], 0, backward_line)
    restored = transform(restored, velocity[1], 1, backward_line)
    restored = transform(restored, velocity[2], 2, backward_line)
    return jnp.stack([restored[(index // 9, (index // 3) % 3, index % 3)] / weights[index]
                      for index in range(27)], 0)


def spread_force(marker_site, marker_frac, marker_force, marker_count):
    slot_index = jnp.arange(MARKERS, dtype=jnp.int32)
    column = slot_index // MCOL
    live_mask = (slot_index % MCOL < marker_count[column]).astype(jnp.float32)
    targets = []
    amounts = []
    for step_x in (0, 1):
        for step_y in (0, 1):
            for step_z in (0, 1):
                factor_x = marker_frac[0] if step_x else 1.0 - marker_frac[0]
                factor_y = marker_frac[1] if step_y else 1.0 - marker_frac[1]
                factor_z = marker_frac[2] if step_z else 1.0 - marker_frac[2]
                weight = live_mask * factor_x * factor_y * factor_z
                cell_x = (column * CX + marker_site[1] + step_x) % NX
                cell_y = (marker_site[0] * CY + marker_site[2] + step_y) % NY
                cell_z = (marker_site[3] + step_z) % NZ
                targets.append(((cell_x * NY + cell_y) * NZ + cell_z).astype(jnp.int32))
                amounts.append(marker_force * weight[None, :])
    field = jnp.zeros((3, NX * NY * NZ), jnp.float32)
    field = field.at[:, jnp.concatenate(targets, 0)].add(jnp.concatenate(amounts, 1))
    return field.reshape(3, NX, NY * NZ)


def reference(populations, marker_site, marker_frac, marker_force, marker_count):
    force = spread_force(marker_site, marker_frac, marker_force, marker_count)

    def one_plane(pair_in):
        return collide(pair_in[0], pair_in[1])

    post = lax.map(one_plane, (jnp.moveaxis(populations, 1, 0), jnp.moveaxis(force, 1, 0)))
    post = jnp.moveaxis(post, 0, 1).reshape(27, NX, NY, NZ)
    read = []
    for index in range(27):
        shift_x = index // 9 - 1
        shift_y = (index // 3) % 3 - 1
        shift_z = index % 3 - 1
        read.append(jnp.roll(post[index], (shift_x, shift_y, shift_z), axis=(0, 1, 2)))
    return jnp.stack(read, 0).reshape(27, NX, NY * NZ)
```

```python
import functools

import jax
import jax.numpy as jnp
from jax import lax
from jax.experimental import pallas as pl
from jax.experimental.pallas import tpu as pltpu
from jax.sharding import PartitionSpec as P

NZ = 64
LANES = 128
RELAX_RATE = 1.8
MESH = pl.DeviceIdType.MESH
F32 = jnp.float32
BF16 = jnp.bfloat16


def backward_line(zeroth, first, second, velocity):
    if zeroth is None:
        low = first
    elif first is None:
        low = zeroth * velocity
    else:
        low = zeroth * velocity + first
    high = None
    if low is not None:
        high = velocity * (low if first is None else low + first)
    if second is not None:
        high = second if high is None else high + second
    if low is None:
        lower = upper = high
    else:
        lower, upper = high - low, high + low
    if high is None:
        centre = 0.5 * zeroth
    elif zeroth is None:
        centre = -0.5 * high
    else:
        centre = 0.5 * (zeroth - high)
    return lower, centre, upper


def backward(grid, velocity, axis):
    result = {}
    for outer in range(3):
        for inner in range(3):
            keys = []
            for slot in range(3):
                key = [outer, inner]
                key.insert(axis, slot)
                keys.append(tuple(key))
            made = backward_line(*[grid.get(key) for key in keys], velocity)
            for key, value in zip(keys, made):
                result[key] = value
    return result


def raw_moments(load):
    rows = []
    for i in range(3):
        sums, diffs, evens = [], [], []
        for j in range(3):
            low, mid, high = load(9 * i + 3 * j), load(9 * i + 3 * j + 1), load(9 * i + 3 * j + 2)
            even = low + high
            evens.append(even)
            sums.append(even + 4.0 * mid)
            diffs.append(high - low)
        even = sums[0] + sums[2]
        rows.append(
            (
                even + 4.0 * sums[1],
                sums[2] - sums[0],
                even,
                diffs[0] + diffs[2] + 4.0 * diffs[1],
                diffs[2] - diffs[0],
                evens[0] + evens[2] + 4.0 * evens[1],
            )
        )

    def total(at):
        return rows[0][at] + rows[2][at] + 4.0 * rows[1][at]

    def first(at):
        return rows[2][at] - rows[0][at]

    made = (
        total(0),
        first(0),
        total(1),
        total(3),
        rows[0][0] + rows[2][0],
        total(2),
        total(5),
        first(1),
        first(3),
        total(4),
    )
    return [value * (1.0 / 216.0) for value in made]


def collided(moments, force):
    density, jx, jy, jz, cxx, cyy, czz, cxy, cxz, cyz = moments
    gx, gy, gz = [0.5 * value for value in force]
    inverse = 1.0 / density
    velocity = ((jx + gx) * inverse, (jy + gy) * inverse, (jz + gz) * inverse)
    cxx = cxx + (gx * gx - jx * jx) * inverse
    cyy = cyy + (gy * gy - jy * jy) * inverse
    czz = czz + (gz * gz - jz * jz) * inverse
    cxy = cxy + (gx * gy - jx * jy) * inverse
    cxz = cxz + (gx * gz - jx * jz) * inverse
    cyz = cyz + (gy * gz - jy * jz) * inverse
    keep = 1.0 - RELAX_RATE
    scaled = keep * inverse
    base = (1.0 / 3.0) - (cxx + cyy + czz) * (scaled * (1.0 / 3.0))
    sxx, syy, szz = base + cxx * scaled, base + cyy * scaled, base + czz * scaled
    sxy, sxz, syz = cxy * scaled, cxz * scaled, cyz * scaled
    mass = 27.0 * density
    dxy, dxz, dyz = 2.0 * sxy, 2.0 * sxz, 2.0 * syz
    pxy = sxx * syy + dxy * sxy
    qxy, qxz, qyz = dxy * sxy, dxz * sxz, dyz * syz
    grid = {
        (0, 0, 0): mass,
        (1, 0, 0): 27.0 * gx,
        (0, 1, 0): 27.0 * gy,
        (0, 0, 1): 27.0 * gz,
        (2, 0, 0): mass * sxx,
        (0, 2, 0): mass * syy,
        (0, 0, 2): mass * szz,
        (1, 1, 0): mass * sxy,
        (1, 0, 1): mass * sxz,
        (0, 1, 1): mass * syz,
        (2, 2, 0): mass * pxy,
        (2, 0, 2): mass * (sxx * szz + qxz),
        (0, 2, 2): mass * (syy * szz + qyz),
        (2, 1, 1): mass * (sxx * syz + dxy * sxz),
        (1, 2, 1): mass * (syy * sxz + dxy * syz),
        (1, 1, 2): mass * (szz * sxy + dxz * syz),
        (2, 2, 2): mass * (pxy * szz + sxx * qyz + syy * qxz + 4.0 * (dxy * (sxz * syz))),
    }
    for axis in range(3):
        grid = backward(grid, velocity[axis], axis)
    return grid


def split(value):
    high = value.astype(BF16).astype(F32)
    return high, value - high


def step_kernel(
    n_x, n_y, pop, site, frac, force, count, out,
    in_v, mom, slots, lhs_hi, lhs_lo, rhs_hi, rhs_lo, acc, rim_s, rim_r, out_v,
    face_p, face_m, got_p, got_m, side_p, side_m, cor,
    in_sem, mark_s, mark_r, rim_sem, face_sem, side_sem, cor_s, cor_r, out_sem,
):
    me_x, me_y = lax.axis_index("gx"), lax.axis_index("gy")
    tiles = in_v.shape[0]
    tile_y = 2 * tiles
    own = site.shape[1]
    right, left = lax.rem(me_x + 1, n_x), lax.rem(me_x + n_x - 1, n_x)
    above, below = lax.rem(me_y + 1, n_y), lax.rem(me_y + n_y - 1, n_y)

    def in_copy(t):
        lanes = pl.ds(pl.multiple_of(t * LANES, LANES), LANES)
        return pltpu.make_async_copy(pop.at[:, :, lanes], in_v.at[t], in_sem.at[t])

    @pl.loop(0, tiles)
    def _(t):
        in_copy(t).start()

    barrier = pltpu.get_barrier_semaphore()
    near = [(me_x, lax.rem(me_y + k, n_y)) for k in range(1, n_y)]
    near += [(a, b) for a in (right, left) for b in (me_y, above, below)]
    for device in near:
        pl.semaphore_signal(barrier, inc=1, device_id=device, device_id_type=MESH)

    rank = me_y * own + lax.broadcasted_iota(jnp.int32, (3, own), 1)
    slots[0, 0:4, :] = site[...].astype(F32)
    slots[0, 4:7, :] = frac[...]
    slots[0, 7:10, :] = jnp.where(rank < count[0], force[...], 0.0)

    pl.semaphore_wait(barrier, len(near))

    def mark_copy(k):
        return pltpu.make_async_remote_copy(
            src_ref=slots.at[0],
            dst_ref=slots.at[k],
            send_sem=mark_s.at[k],
            recv_sem=mark_r.at[k],
            device_id=(me_x, lax.rem(me_y + k, n_y)),
            device_id_type=MESH,
        )

    for k in range(1, n_y):
        mark_copy(k).start()

    def spread(k):
        def row(at):
            return jnp.broadcast_to(slots[k, at : at + 1, :], (8, own))

        cells = lax.broadcasted_iota(jnp.int32, (8, own), 0).astype(F32)
        at_y = row(0) * float(tile_y) + row(2) - (me_y * tile_y).astype(F32)
        at_y = jnp.where(at_y < 0.0, at_y + float(tile_y * n_y), at_y)
        next_y = at_y + 1.0
        next_y = jnp.where(next_y == float(tile_y * n_y), 0.0, next_y)
        at_x, at_z = row(1), row(3)
        next_z = jnp.where(at_z == NZ - 1.0, 0.0, at_z + 1.0)
        frac_x, frac_y, frac_z = row(4), row(5), row(6)
        weight_x = jnp.where(
            cells == at_x, 1.0 - frac_x, jnp.where(cells == at_x + 1.0, frac_x, 0.0)
        )
        first = split(weight_x * (1.0 - frac_y))
        second = split(weight_x * frac_y)
        refs = (lhs_hi, lhs_lo)
        for pair in range(tile_y // 2):
            picked = [[], []]
            for y in (2 * pair, 2 * pair + 1):
                hit, hit_next = at_y == float(y), next_y == float(y)
                for part in range(2):
                    picked[part].append(
                        jnp.where(hit, first[part], jnp.where(hit_next, second[part], 0.0))
                    )
            for part in range(2):
                refs[part][16 * pair : 16 * pair + 16, :] = jnp.concatenate(picked[part], 0).astype(BF16)
        rim = jnp.where(at_x == 7.0, frac_x, 0.0)
        first = split(rim * (1.0 - frac_y))
        second = split(rim * frac_y)
        for pair in range(tile_y // 16):
            picked = [[], []]
            for half in range(2):
                rows = cells + float(16 * pair + 8 * half)
                hit, hit_next = at_y == rows, next_y == rows
                for part in range(2):
                    picked[part].append(
                        jnp.where(hit, first[part], jnp.where(hit_next, second[part], 0.0))
                    )
            base = 8 * tile_y + 16 * pair
            for part in range(2):
                refs[part][base : base + 16, :] = jnp.concatenate(picked[part], 0).astype(BF16)
        refs = (rhs_hi, rhs_lo)
        for axis in range(3):
            amount = row(7 + axis)
            first = split(amount * (1.0 - frac_z))
            second = split(amount * frac_z)
            for pair in range(NZ // 16):
                picked = [[], []]
                for half in range(2):
                    rows = cells + float(16 * pair + 8 * half)
                    hit, hit_next = at_z == rows, next_z == rows
                    for part in range(2):
                        picked[part].append(
                            jnp.where(hit, first[part], jnp.where(hit_next, second[part], 0.0))
                        )
                base = axis * NZ + 16 * pair
                for part in range(2):
                    refs[part][base : base + 16, :] = jnp.concatenate(picked[part], 0).astype(BF16)

        def product(a, b):
            return lax.dot_general(
                a[...], b[...], (((1,), (1,)), ((), ())), preferred_element_type=F32
            )

        return product(lhs_hi, rhs_hi) + product(lhs_hi, rhs_lo) + product(lhs_lo, rhs_hi)

    width = 3 * NZ
    acc[:, 0:width] = spread(0)

    @pl.loop(1, n_y)
    def _(k):
        mark_copy(k).wait_recv()
        acc[:, 0:width] += spread(k)

    rim_s[...] = acc[8 * tile_y :, :]
    rim_copy = pltpu.make_async_remote_copy(
        src_ref=rim_s, dst_ref=rim_r, send_sem=rim_sem.at[0], recv_sem=rim_sem.at[1],
        device_id=(right, me_y), device_id_type=MESH,
    )
    rim_copy.start()

    @pl.loop(0, tiles)
    def _(t):
        in_copy(t).wait()
        for at, value in enumerate(raw_moments(lambda q: in_v[t, q])):
            mom[t, at] = value

    rim_copy.wait_recv()
    for y in range(tile_y):
        acc[8 * y : 8 * y + 1, :] += rim_r[y : y + 1, :]

    lane = lax.broadcasted_iota(jnp.int32, (8, LANES), 1)
    lower_half = lane < NZ
    z_low = (lane == 0) | (lane == NZ)
    z_high = (lane == NZ - 1) | (lane == LANES - 1)

    @pl.loop(0, tiles)
    def _(t):
        even = acc[pl.ds(pl.multiple_of(16 * t, 16), 8), :]
        odd = acc[pl.ds(pl.multiple_of(16 * t + 8, 8), 8), :]
        a0, a1, b0, b1 = even[:, :LANES], even[:, LANES:], odd[:, :LANES], odd[:, LANES:]
        forces = (
            jnp.where(lower_half, a0, pltpu.roll(b0, NZ, 1)),
            jnp.where(lower_half, pltpu.roll(a0, NZ, 1), b0),
            jnp.where(lower_half, a1, pltpu.roll(b1, NZ, 1)),
        )
        post = collided([mom[t, at] for at in range(10)], forces)
        for i in range(3):
            for j in range(3):
                for k in range(3):
                    q = 9 * i + 3 * j + k
                    value = post[i, j, k]
                    if k == 1:
                        if j != 1:
                            value = pltpu.roll(value, NZ, 1)
                    else:
                        near_by, edge, far = (1, z_low, NZ + 1) if k == 2 else (LANES - 1, z_high, NZ - 1)
                        plain, wrapped = pltpu.roll(value, near_by, 1), pltpu.roll(value, far, 1)
                        if j != 1:
                            plain, wrapped = wrapped, plain
                        value = jnp.where(edge, wrapped, plain)
                    moved = value
                    if i == 2:
                        moved = pltpu.roll(value, 1, 0)
                    elif i == 0:
                        moved = pltpu.roll(value, 7, 0)
                    line = moved if i == 2 else value
                    face = (face_m, None, face_p)[i]
                    at = 3 * j + k
                    if j == 1:
                        out_v[q, t + 1] = moved
                        if i != 1:
                            face[t + 1, at : at + 1, :] = line[0:1, :]
                    else:
                        low_at, high_at = (t + 2, t + 1) if j == 2 else (t + 1, t)
                        out_v[q, low_at, :, 0:NZ] = moved[:, 0:NZ]
                        out_v[q, high_at, :, NZ:] = moved[:, NZ:]
                        if i != 1:
                            face[low_at, at : at + 1, 0:NZ] = line[0:1, 0:NZ]
                            face[high_at, at : at + 1, NZ:] = line[0:1, NZ:]

    def send(src, dst, sems, device):
        return pltpu.make_async_remote_copy(
            src_ref=src, dst_ref=dst, send_sem=sems[0], recv_sem=sems[1],
            device_id=device, device_id_type=MESH,
        )

    inner = pl.ds(1, tiles)
    faces = [
        send(face_p.at[inner], got_p, (face_sem.at[0], face_sem.at[1]), (right, me_y)),
        send(face_m.at[inner], got_m, (face_sem.at[2], face_sem.at[3]), (left, me_y)),
    ]
    corners = []
    for at, (buffer, tile, device) in enumerate(
        (
            (face_p, tiles + 1, (right, above)),
            (face_p, 0, (right, below)),
            (face_m, tiles + 1, (left, above)),
            (face_m, 0, (left, below)),
        )
    ):
        corners.append(send(buffer.at[tile], cor.at[at], (cor_s.at[at], cor_r.at[at]), device))
    sides = []
    for i in range(3):
        sides.append(
            send(out_v.at[pl.ds(9 * i + 6, 3), tiles + 1], side_p.at[pl.ds(3 * i, 3)],
                 (side_sem.at[0, i], side_sem.at[1, i]), (me_x, above))
        )
        sides.append(
            send(out_v.at[pl.ds(9 * i, 3), 0], side_m.at[pl.ds(3 * i, 3)],
                 (side_sem.at[2, i], side_sem.at[3, i]), (me_x, below))
        )
    for copy in faces + corners + sides:
        copy.start()

    for copy in sides:
        copy.wait_recv()
    for i in range(3):
        for k in range(3):
            out_v[9 * i + 6 + k, 1, :, 0:NZ] = side_p[3 * i + k, :, 0:NZ]
            out_v[9 * i + k, tiles, :, NZ:] = side_m[3 * i + k, :, NZ:]

    def out_copy(t, group):
        lanes = pl.ds(pl.multiple_of(t * LANES, LANES), LANES)
        rows = pl.ds(9 * group, 9)
        return pltpu.make_async_copy(
            out_v.at[rows, t + 1], out.at[rows, :, lanes], out_sem.at[group, t]
        )

    @pl.loop(0, tiles)
    def _(t):
        out_copy(t, 1).start()

    for copy in corners:
        copy.wait_recv()
    for copy in faces:
        copy.wait_recv()
    for k in range(3):
        got_p[0, 6 + k : 7 + k, 0:NZ] = cor[0, 6 + k : 7 + k, 0:NZ]
        got_p[tiles - 1, k : k + 1, NZ:] = cor[1, k : k + 1, NZ:]
        got_m[0, 6 + k : 7 + k, 0:NZ] = cor[2, 6 + k : 7 + k, 0:NZ]
        got_m[tiles - 1, k : k + 1, NZ:] = cor[3, k : k + 1, NZ:]

    @pl.loop(0, tiles)
    def _(t):
        for at in range(9):
            out_v[18 + at, t + 1, 0:1, :] = got_p[t, at : at + 1, :]
            out_v[at, t + 1, 7:8, :] = got_m[t, at : at + 1, :]
        out_copy(t, 0).start()
        out_copy(t, 2).start()

    for k in range(1, n_y):
        mark_copy(k).wait_send()
    rim_copy.wait_send()
    for copy in faces + corners + sides:
        copy.wait_send()

    @pl.loop(0, tiles)
    def _(t):
        for group in range(3):
            out_copy(t, group).wait()


def per_device(n_x, n_y, populations, marker_site, marker_frac, marker_force, marker_count):
    tiles = populations.shape[2] // LANES
    own = marker_site.shape[1]
    tile_y = 2 * tiles
    rows = 9 * tile_y
    width = 3 * NZ
    dma = pltpu.SemaphoreType.DMA
    vmem = pl.BlockSpec(memory_space=pltpu.VMEM)
    anywhere = pl.BlockSpec(memory_space=pl.ANY)
    return pl.pallas_call(
        functools.partial(step_kernel, n_x, n_y),
        out_shape=jax.ShapeDtypeStruct(populations.shape, F32),
        in_specs=[anywhere, vmem, vmem, vmem, pl.BlockSpec(memory_space=pltpu.SMEM)],
        out_specs=anywhere,
        scratch_shapes=[
            pltpu.VMEM((tiles, 27, 8, LANES), F32),
            pltpu.VMEM((tiles, 10, 8, LANES), F32),
            pltpu.VMEM((n_y, 10, own), F32),
            pltpu.VMEM((rows, own), BF16),
            pltpu.VMEM((rows, own), BF16),
            pltpu.VMEM((width, own), BF16),
            pltpu.VMEM((width, own), BF16),
            pltpu.VMEM((rows, 2 * LANES), F32),
            pltpu.VMEM((tile_y, 2 * LANES), F32),
            pltpu.VMEM((tile_y, 2 * LANES), F32),
            pltpu.VMEM((27, tiles + 2, 8, LANES), F32),
            pltpu.VMEM((tiles + 2, 9, LANES), F32),
            pltpu.VMEM((tiles + 2, 9, LANES), F32),
            pltpu.VMEM((tiles, 9, LANES), F32),
            pltpu.VMEM((tiles, 9, LANES), F32),
            pltpu.VMEM((9, 8, LANES), F32),
            pltpu.VMEM((9, 8, LANES), F32),
            pltpu.VMEM((4, 9, LANES), F32),
            dma((tiles,)),
            dma((n_y,)),
            dma((n_y,)),
            dma((2,)),
            dma((4,)),
            dma((4, 3)),
            dma((4,)),
            dma((4,)),
            dma((3, tiles)),
        ],
        compiler_params=pltpu.CompilerParams(
            collective_id=0, has_side_effects=True, vmem_limit_bytes=40 * 1024 * 1024
        ),
    )(populations, marker_site, marker_frac, marker_force, marker_count)


def solution(mesh):
    in_specs = (
        P(None, "gx", "gy"),
        P(None, ("gx", "gy")),
        P(None, ("gx", "gy")),
        P(None, ("gx", "gy")),
        P("gx"),
    )
    return jax.shard_map(
        functools.partial(per_device, mesh.shape["gx"], mesh.shape["gy"]),
        mesh=mesh,
        in_specs=in_specs,
        out_specs=P(None, "gx", "gy"),
        check_vma=False,
    )
```

```python
import functools

import jax
import jax.numpy as jnp
from jax import lax
from jax.experimental import pallas as pl
from jax.experimental.pallas import tpu as pltpu
from jax.sharding import PartitionSpec as P

NZ = 64
LANES = 128
RELAX_RATE = 1.8
MESH = pl.DeviceIdType.MESH
F32 = jnp.float32
BF16 = jnp.bfloat16


def backward_line(zeroth, first, second, velocity):
    if zeroth is None:
        low = first
    elif first is None:
        low = zeroth * velocity
    else:
        low = zeroth * velocity + first
    high = None
    if low is not None:
        high = velocity * (low if first is None else low + first)
    if second is not None:
        high = second if high is None else high + second
    if low is None:
        lower = upper = high
    else:
        lower, upper = high - low, high + low
    if high is None:
        centre = 0.5 * zeroth
    elif zeroth is None:
        centre = -0.5 * high
    else:
        centre = 0.5 * (zeroth - high)
    return lower, centre, upper


def backward(grid, velocity, axis):
    result = {}
    for outer in range(3):
        for inner in range(3):
            keys = []
            for slot in range(3):
                key = [outer, inner]
                key.insert(axis, slot)
                keys.append(tuple(key))
            made = backward_line(*[grid.get(key) for key in keys], velocity)
            for key, value in zip(keys, made):
                result[key] = value
    return result


def raw_moments(load):
    rows = []
    for i in range(3):
        sums, diffs, evens = [], [], []
        for j in range(3):
            low, mid, high = load(9 * i + 3 * j), load(9 * i + 3 * j + 1), load(9 * i + 3 * j + 2)
            even = low + high
            evens.append(even)
            sums.append(even + 4.0 * mid)
            diffs.append(high - low)
        even = sums[0] + sums[2]
        rows.append(
            (
                even + 4.0 * sums[1],
                sums[2] - sums[0],
                even,
                diffs[0] + diffs[2] + 4.0 * diffs[1],
                diffs[2] - diffs[0],
                evens[0] + evens[2] + 4.0 * evens[1],
            )
        )

    def total(at):
        return rows[0][at] + rows[2][at] + 4.0 * rows[1][at]

    def first(at):
        return rows[2][at] - rows[0][at]

    made = (
        total(0),
        first(0),
        total(1),
        total(3),
        rows[0][0] + rows[2][0],
        total(2),
        total(5),
        first(1),
        first(3),
        total(4),
    )
    return [value * (1.0 / 216.0) for value in made]


def collided(moments, force):
    density, jx, jy, jz, cxx, cyy, czz, cxy, cxz, cyz = moments
    gx, gy, gz = [0.5 * value for value in force]
    inverse = 1.0 / density
    velocity = ((jx + gx) * inverse, (jy + gy) * inverse, (jz + gz) * inverse)
    cxx = cxx + (gx * gx - jx * jx) * inverse
    cyy = cyy + (gy * gy - jy * jy) * inverse
    czz = czz + (gz * gz - jz * jz) * inverse
    cxy = cxy + (gx * gy - jx * jy) * inverse
    cxz = cxz + (gx * gz - jx * jz) * inverse
    cyz = cyz + (gy * gz - jy * jz) * inverse
    keep = 1.0 - RELAX_RATE
    scaled = keep * inverse
    base = (1.0 / 3.0) - (cxx + cyy + czz) * (scaled * (1.0 / 3.0))
    sxx, syy, szz = base + cxx * scaled, base + cyy * scaled, base + czz * scaled
    sxy, sxz, syz = cxy * scaled, cxz * scaled, cyz * scaled
    mass = 27.0 * density
    dxy, dxz, dyz = 2.0 * sxy, 2.0 * sxz, 2.0 * syz
    pxy = sxx * syy + dxy * sxy
    qxy, qxz, qyz = dxy * sxy, dxz * sxz, dyz * syz
    grid = {
        (0, 0, 0): mass,
        (1, 0, 0): 27.0 * gx,
        (0, 1, 0): 27.0 * gy,
        (0, 0, 1): 27.0 * gz,
        (2, 0, 0): mass * sxx,
        (0, 2, 0): mass * syy,
        (0, 0, 2): mass * szz,
        (1, 1, 0): mass * sxy,
        (1, 0, 1): mass * sxz,
        (0, 1, 1): mass * syz,
        (2, 2, 0): mass * pxy,
        (2, 0, 2): mass * (sxx * szz + qxz),
        (0, 2, 2): mass * (syy * szz + qyz),
        (2, 1, 1): mass * (sxx * syz + dxy * sxz),
        (1, 2, 1): mass * (syy * sxz + dxy * syz),
        (1, 1, 2): mass * (szz * sxy + dxz * syz),
        (2, 2, 2): mass * (pxy * szz + sxx * qyz + syy * qxz + 4.0 * (dxy * (sxz * syz))),
    }
    for axis in range(3):
        grid = backward(grid, velocity[axis], axis)
    return grid


def split(value):
    high = value.astype(BF16).astype(F32)
    return high, value - high


def step_kernel(
    n_x, n_y, pop, site_h, frac_h, force_h, count, out,
    site, frac, force, in_v, mom, slots, lhs_hi, lhs_lo, rhs_hi, rhs_lo, acc, rim_s, rim_r, out_v,
    face_p, face_m, got_p, got_m, side_p, side_m, cor,
    own_sem, in_sem, mark_s, mark_r, rim_sem, face_sem, side_sem, cor_s, cor_r, out_sem,
):
    me_x, me_y = lax.axis_index("gx"), lax.axis_index("gy")
    tiles = in_v.shape[0]
    tile_y = 2 * tiles
    own = site.shape[1]
    right, left = lax.rem(me_x + 1, n_x), lax.rem(me_x + n_x - 1, n_x)
    above, below = lax.rem(me_y + 1, n_y), lax.rem(me_y + n_y - 1, n_y)

    def in_copy(t):
        lanes = pl.ds(pl.multiple_of(t * LANES, LANES), LANES)
        return pltpu.make_async_copy(pop.at[:, :, lanes], in_v.at[t], in_sem.at[t])

    fetches = [
        pltpu.make_async_copy(src, dst, own_sem.at[at])
        for at, (src, dst) in enumerate(((site_h, site), (frac_h, frac), (force_h, force)))
    ]
    for copy in fetches:
        copy.start()

    barrier = pltpu.get_barrier_semaphore()
    near = [(me_x, lax.rem(me_y + k, n_y)) for k in range(1, n_y)]
    near += [(a, b) for a in (right, left) for b in (me_y, above, below)]
    for device in near:
        pl.semaphore_signal(barrier, inc=1, device_id=device, device_id_type=MESH)

    @pl.loop(0, tiles)
    def _(t):
        in_copy(t).start()

    for copy in fetches:
        copy.wait()
    rank = me_y * own + lax.broadcasted_iota(jnp.int32, (3, own), 1)
    slots[0, 0:4, :] = site[...].astype(F32)
    slots[0, 4:7, :] = frac[...]
    slots[0, 7:10, :] = jnp.where(rank < count[0], force[...], 0.0)

    pl.semaphore_wait(barrier, len(near))

    def mark_copy(k):
        return pltpu.make_async_remote_copy(
            src_ref=slots.at[0],
            dst_ref=slots.at[k],
            send_sem=mark_s.at[k],
            recv_sem=mark_r.at[k],
            device_id=(me_x, lax.rem(me_y + k, n_y)),
            device_id_type=MESH,
        )

    for k in range(1, n_y):
        mark_copy(k).start()

    def spread(k):
        def row(at):
            return jnp.broadcast_to(slots[k, at : at + 1, :], (8, own))

        cells = lax.broadcasted_iota(jnp.int32, (8, own), 0).astype(F32)
        at_y = row(0) * float(tile_y) + row(2) - (me_y * tile_y).astype(F32)
        at_y = jnp.where(at_y < 0.0, at_y + float(tile_y * n_y), at_y)
        next_y = at_y + 1.0
        next_y = jnp.where(next_y == float(tile_y * n_y), 0.0, next_y)
        at_x, at_z = row(1), row(3)
        next_z = jnp.where(at_z == NZ - 1.0, 0.0, at_z + 1.0)
        frac_x, frac_y, frac_z = row(4), row(5), row(6)
        weight_x = jnp.where(
            cells == at_x, 1.0 - frac_x, jnp.where(cells == at_x + 1.0, frac_x, 0.0)
        )
        first = split(weight_x * (1.0 - frac_y))
        second = split(weight_x * frac_y)
        refs = (lhs_hi, lhs_lo)
        for pair in range(tile_y // 2):
            picked = [[], []]
            for y in (2 * pair, 2 * pair + 1):
                hit, hit_next = at_y == float(y), next_y == float(y)
                for part in range(2):
                    picked[part].append(
                        jnp.where(hit, first[part], jnp.where(hit_next, second[part], 0.0))
                    )
            for part in range(2):
                refs[part][16 * pair : 16 * pair + 16, :] = jnp.concatenate(picked[part], 0).astype(BF16)
        rim = jnp.where(at_x == 7.0, frac_x, 0.0)
        first = split(rim * (1.0 - frac_y))
        second = split(rim * frac_y)
        for pair in range(tile_y // 16):
            picked = [[], []]
            for half in range(2):
                rows = cells + float(16 * pair + 8 * half)
                hit, hit_next = at_y == rows, next_y == rows
                for part in range(2):
                    picked[part].append(
                        jnp.where(hit, first[part], jnp.where(hit_next, second[part], 0.0))
                    )
            base = 8 * tile_y + 16 * pair
            for part in range(2):
                refs[part][base : base + 16, :] = jnp.concatenate(picked[part], 0).astype(BF16)
        refs = (rhs_hi, rhs_lo)
        for axis in range(3):
            amount = row(7 + axis)
            first = split(amount * (1.0 - frac_z))
            second = split(amount * frac_z)
            for pair in range(NZ // 16):
                picked = [[], []]
                for half in range(2):
                    rows = cells + float(16 * pair + 8 * half)
                    hit, hit_next = at_z == rows, next_z == rows
                    for part in range(2):
                        picked[part].append(
                            jnp.where(hit, first[part], jnp.where(hit_next, second[part], 0.0))
                        )
                base = axis * NZ + 16 * pair
                for part in range(2):
                    refs[part][base : base + 16, :] = jnp.concatenate(picked[part], 0).astype(BF16)

        def product(a, b):
            return lax.dot_general(
                a[...], b[...], (((1,), (1,)), ((), ())), preferred_element_type=F32
            )

        return product(lhs_hi, rhs_hi) + product(lhs_hi, rhs_lo) + product(lhs_lo, rhs_hi)

    width = 3 * NZ
    acc[:, 0:width] = spread(0)

    @pl.loop(1, n_y)
    def _(k):
        mark_copy(k).wait_recv()
        acc[:, 0:width] += spread(k)

    rim_s[...] = acc[8 * tile_y :, :]
    rim_copy = pltpu.make_async_remote_copy(
        src_ref=rim_s, dst_ref=rim_r, send_sem=rim_sem.at[0], recv_sem=rim_sem.at[1],
        device_id=(right, me_y), device_id_type=MESH,
    )
    rim_copy.start()

    @pl.loop(0, tiles)
    def _(t):
        in_copy(t).wait()
        for at, value in enumerate(raw_moments(lambda q: in_v[t, q])):
            mom[t, at] = value

    rim_copy.wait_recv()
    for y in range(tile_y):
        acc[8 * y : 8 * y + 1, :] += rim_r[y : y + 1, :]

    lane = lax.broadcasted_iota(jnp.int32, (8, LANES), 1)
    lower_half = lane < NZ
    z_low = (lane == 0) | (lane == NZ)
    z_high = (lane == NZ - 1) | (lane == LANES - 1)

    def tile_step(t):
        even = acc[pl.ds(pl.multiple_of(16 * t, 16), 8), :]
        odd = acc[pl.ds(pl.multiple_of(16 * t + 8, 8), 8), :]
        a0, a1, b0, b1 = even[:, :LANES], even[:, LANES:], odd[:, :LANES], odd[:, LANES:]
        forces = (
            jnp.where(lower_half, a0, pltpu.roll(b0, NZ, 1)),
            jnp.where(lower_half, pltpu.roll(a0, NZ, 1), b0),
            jnp.where(lower_half, a1, pltpu.roll(b1, NZ, 1)),
        )
        post = collided([mom[t, at] for at in range(10)], forces)
        for i in range(3):
            for j in range(3):
                for k in range(3):
                    q = 9 * i + 3 * j + k
                    value = post[i, j, k]
                    if k == 1:
                        if j != 1:
                            value = pltpu.roll(value, NZ, 1)
                    else:
                        near_by, edge, far = (1, z_low, NZ + 1) if k == 2 else (LANES - 1, z_high, NZ - 1)
                        plain, wrapped = pltpu.roll(value, near_by, 1), pltpu.roll(value, far, 1)
                        if j != 1:
                            plain, wrapped = wrapped, plain
                        value = jnp.where(edge, wrapped, plain)
                    moved = value
                    if i == 2:
                        moved = pltpu.roll(value, 1, 0)
                    elif i == 0:
                        moved = pltpu.roll(value, 7, 0)
                    line = moved if i == 2 else value
                    face = (face_m, None, face_p)[i]
                    at = 3 * j + k
                    if j == 1:
                        out_v[q, t + 1] = moved
                        if i != 1:
                            face[t + 1, at : at + 1, :] = line[0:1, :]
                    else:
                        low_at, high_at = (t + 2, t + 1) if j == 2 else (t + 1, t)
                        out_v[q, low_at, :, 0:NZ] = moved[:, 0:NZ]
                        out_v[q, high_at, :, NZ:] = moved[:, NZ:]
                        if i != 1:
                            face[low_at, at : at + 1, 0:NZ] = line[0:1, 0:NZ]
                            face[high_at, at : at + 1, NZ:] = line[0:1, NZ:]

    def send(src, dst, sems, device):
        return pltpu.make_async_remote_copy(
            src_ref=src, dst_ref=dst, send_sem=sems[0], recv_sem=sems[1],
            device_id=device, device_id_type=MESH,
        )

    corners = []
    for at, (buffer, tile, device) in enumerate(
        (
            (face_p, tiles + 1, (right, above)),
            (face_p, 0, (right, below)),
            (face_m, tiles + 1, (left, above)),
            (face_m, 0, (left, below)),
        )
    ):
        corners.append(send(buffer.at[tile], cor.at[at], (cor_s.at[at], cor_r.at[at]), device))
    sides = []
    for i in range(3):
        sides.append(
            send(out_v.at[pl.ds(9 * i + 6, 3), tiles + 1], side_p.at[pl.ds(3 * i, 3)],
                 (side_sem.at[0, i], side_sem.at[1, i]), (me_x, above))
        )
        sides.append(
            send(out_v.at[pl.ds(9 * i, 3), 0], side_m.at[pl.ds(3 * i, 3)],
                 (side_sem.at[2, i], side_sem.at[3, i]), (me_x, below))
        )
    @pl.loop(0, 2)
    def _(end):
        tile_step(end * (tiles - 1))

    for copy in corners + sides:
        copy.start()

    faces = []
    begin, source = 1, 1
    for part in range(3):
        stop = 1 + (part + 1) * (tiles - 2) // 3

        @pl.loop(begin, stop)
        def _(t):
            tile_step(t)

        end = tiles + 1 if part == 2 else stop
        rows, places = pl.ds(source, end - source), pl.ds(source - 1, end - source)
        for at, (buffer, got, device) in enumerate(
            ((face_p, got_p, (right, me_y)), (face_m, got_m, (left, me_y)))
        ):
            sems = (face_sem.at[2 * at, part], face_sem.at[2 * at + 1, part])
            faces.append(send(buffer.at[rows], got.at[places], sems, device))
        faces[-2].start()
        faces[-1].start()
        begin, source = stop, end

    for copy in sides:
        copy.wait_recv()
    for i in range(3):
        for k in range(3):
            out_v[9 * i + 6 + k, 1, :, 0:NZ] = side_p[3 * i + k, :, 0:NZ]
            out_v[9 * i + k, tiles, :, NZ:] = side_m[3 * i + k, :, NZ:]

    def out_copy(t, group):
        lanes = pl.ds(pl.multiple_of(t * LANES, LANES), LANES)
        rows = pl.ds(9 * group, 9)
        return pltpu.make_async_copy(
            out_v.at[rows, t + 1], out.at[rows, :, lanes], out_sem.at[group, t]
        )

    @pl.loop(0, tiles)
    def _(t):
        for group in range(3):
            out_copy(t, group).start()

    @pl.loop(0, tiles)
    def _(t):
        for group in range(3):
            out_copy(t, group).wait()

    for copy in corners:
        copy.wait_recv()
    for copy in faces:
        copy.wait_recv()
    for k in range(3):
        got_p[0, 6 + k : 7 + k, 0:NZ] = cor[0, 6 + k : 7 + k, 0:NZ]
        got_p[tiles - 1, k : k + 1, NZ:] = cor[1, k : k + 1, NZ:]
        got_m[0, 6 + k : 7 + k, 0:NZ] = cor[2, 6 + k : 7 + k, 0:NZ]
        got_m[tiles - 1, k : k + 1, NZ:] = cor[3, k : k + 1, NZ:]

    @pl.loop(0, tiles)
    def _(t):
        lanes = pl.ds(pl.multiple_of(t * LANES, LANES), LANES)
        for at in range(9):
            out[18 + at, 0:1, lanes] = got_p[t, at : at + 1, :]
            out[at, 7:8, lanes] = got_m[t, at : at + 1, :]

    for k in range(1, n_y):
        mark_copy(k).wait_send()
    rim_copy.wait_send()
    for copy in faces + corners + sides:
        copy.wait_send()


def per_device(n_x, n_y, populations, marker_site, marker_frac, marker_force, marker_count):
    tiles = populations.shape[2] // LANES
    own = marker_site.shape[1]
    tile_y = 2 * tiles
    rows = 9 * tile_y
    width = 3 * NZ
    dma = pltpu.SemaphoreType.DMA
    hbm = pl.BlockSpec(memory_space=pltpu.HBM)
    return pl.pallas_call(
        functools.partial(step_kernel, n_x, n_y),
        out_shape=jax.ShapeDtypeStruct(populations.shape, F32),
        in_specs=[hbm, hbm, hbm, hbm, pl.BlockSpec(memory_space=pltpu.SMEM)],
        out_specs=pl.BlockSpec(memory_space=pltpu.VMEM),
        scratch_shapes=[
            pltpu.VMEM((4, own), jnp.int32),
            pltpu.VMEM((3, own), F32),
            pltpu.VMEM((3, own), F32),
            pltpu.VMEM((tiles, 27, 8, LANES), F32),
            pltpu.VMEM((tiles, 10, 8, LANES), F32),
            pltpu.VMEM((n_y, 10, own), F32),
            pltpu.VMEM((rows, own), BF16),
            pltpu.VMEM((rows, own), BF16),
            pltpu.VMEM((width, own), BF16),
            pltpu.VMEM((width, own), BF16),
            pltpu.VMEM((rows, 2 * LANES), F32),
            pltpu.VMEM((tile_y, 2 * LANES), F32),
            pltpu.VMEM((tile_y, 2 * LANES), F32),
            pltpu.VMEM((27, tiles + 2, 8, LANES), F32),
            pltpu.VMEM((tiles + 2, 9, LANES), F32),
            pltpu.VMEM((tiles + 2, 9, LANES), F32),
            pltpu.VMEM((tiles, 9, LANES), F32),
            pltpu.VMEM((tiles, 9, LANES), F32),
            pltpu.VMEM((9, 8, LANES), F32),
            pltpu.VMEM((9, 8, LANES), F32),
            pltpu.VMEM((4, 9, LANES), F32),
            dma((3,)),
            dma((tiles,)),
            dma((n_y,)),
            dma((n_y,)),
            dma((2,)),
            dma((4, 3)),
            dma((4, 3)),
            dma((4,)),
            dma((4,)),
            dma((3, tiles)),
        ],
        compiler_params=pltpu.CompilerParams(
            collective_id=0, has_side_effects=True, vmem_limit_bytes=40 * 1024 * 1024
        ),
    )(*[pltpu.with_memory_space_constraint(value, pltpu.HBM) for value in (populations, marker_site, marker_frac, marker_force)], marker_count)


def solution(mesh):
    in_specs = (
        P(None, "gx", "gy"),
        P(None, ("gx", "gy")),
        P(None, ("gx", "gy")),
        P(None, ("gx", "gy")),
        P("gx"),
    )
    return jax.shard_map(
        functools.partial(per_device, mesh.shape["gx"], mesh.shape["gy"]),
        mesh=mesh,
        in_specs=in_specs,
        out_specs=P(None, "gx", "gy"),
        check_vma=False,
    )
```

```python
import functools

import jax
import jax.numpy as jnp
from jax import lax
from jax.experimental import pallas as pl
from jax.experimental.pallas import tpu as pltpu
from jax.sharding import PartitionSpec as P

NZ = 64
LANES = 128
RELAX_RATE = 1.8
MESH = pl.DeviceIdType.MESH
F32 = jnp.float32
BF16 = jnp.bfloat16


def backward_line(zeroth, first, second, velocity):
    if zeroth is None:
        low = first
    elif first is None:
        low = zeroth * velocity
    else:
        low = zeroth * velocity + first
    high = None
    if low is not None:
        high = velocity * (low if first is None else low + first)
    if second is not None:
        high = second if high is None else high + second
    if low is None:
        lower = upper = high
    else:
        lower, upper = high - low, high + low
    if high is None:
        centre = 0.5 * zeroth
    elif zeroth is None:
        centre = -0.5 * high
    else:
        centre = 0.5 * (zeroth - high)
    return lower, centre, upper


def backward(grid, velocity, axis):
    result = {}
    for outer in range(3):
        for inner in range(3):
            keys = []
            for slot in range(3):
                key = [outer, inner]
                key.insert(axis, slot)
                keys.append(tuple(key))
            made = backward_line(*[grid.get(key) for key in keys], velocity)
            for key, value in zip(keys, made):
                result[key] = value
    return result


def raw_moments(load):
    rows = []
    for i in range(3):
        sums, diffs, evens = [], [], []
        for j in range(3):
            low, mid, high = load(9 * i + 3 * j), load(9 * i + 3 * j + 1), load(9 * i + 3 * j + 2)
            even = low + high
            evens.append(even)
            sums.append(even + 4.0 * mid)
            diffs.append(high - low)
        even = sums[0] + sums[2]
        rows.append(
            (
                even + 4.0 * sums[1],
                sums[2] - sums[0],
                even,
                diffs[0] + diffs[2] + 4.0 * diffs[1],
                diffs[2] - diffs[0],
                evens[0] + evens[2] + 4.0 * evens[1],
            )
        )

    def total(at):
        return rows[0][at] + rows[2][at] + 4.0 * rows[1][at]

    def first(at):
        return rows[2][at] - rows[0][at]

    made = (
        total(0),
        first(0),
        total(1),
        total(3),
        rows[0][0] + rows[2][0],
        total(2),
        total(5),
        first(1),
        first(3),
        total(4),
    )
    return [value * (1.0 / 216.0) for value in made]


def collided(moments, force):
    density, jx, jy, jz, cxx, cyy, czz, cxy, cxz, cyz = moments
    gx, gy, gz = [0.5 * value for value in force]
    inverse = 1.0 / density
    velocity = ((jx + gx) * inverse, (jy + gy) * inverse, (jz + gz) * inverse)
    cxx = cxx + (gx * gx - jx * jx) * inverse
    cyy = cyy + (gy * gy - jy * jy) * inverse
    czz = czz + (gz * gz - jz * jz) * inverse
    cxy = cxy + (gx * gy - jx * jy) * inverse
    cxz = cxz + (gx * gz - jx * jz) * inverse
    cyz = cyz + (gy * gz - jy * jz) * inverse
    keep = 1.0 - RELAX_RATE
    scaled = keep * inverse
    base = (1.0 / 3.0) - (cxx + cyy + czz) * (scaled * (1.0 / 3.0))
    sxx, syy, szz = base + cxx * scaled, base + cyy * scaled, base + czz * scaled
    sxy, sxz, syz = cxy * scaled, cxz * scaled, cyz * scaled
    mass = 27.0 * density
    dxy, dxz, dyz = 2.0 * sxy, 2.0 * sxz, 2.0 * syz
    pxy = sxx * syy + dxy * sxy
    qxy, qxz, qyz = dxy * sxy, dxz * sxz, dyz * syz
    grid = {
        (0, 0, 0): mass,
        (1, 0, 0): 27.0 * gx,
        (0, 1, 0): 27.0 * gy,
        (0, 0, 1): 27.0 * gz,
        (2, 0, 0): mass * sxx,
        (0, 2, 0): mass * syy,
        (0, 0, 2): mass * szz,
        (1, 1, 0): mass * sxy,
        (1, 0, 1): mass * sxz,
        (0, 1, 1): mass * syz,
        (2, 2, 0): mass * pxy,
        (2, 0, 2): mass * (sxx * szz + qxz),
        (0, 2, 2): mass * (syy * szz + qyz),
        (2, 1, 1): mass * (sxx * syz + dxy * sxz),
        (1, 2, 1): mass * (syy * sxz + dxy * syz),
        (1, 1, 2): mass * (szz * sxy + dxz * syz),
        (2, 2, 2): mass * (pxy * szz + sxx * qyz + syy * qxz + 4.0 * (dxy * (sxz * syz))),
    }
    for axis in range(3):
        grid = backward(grid, velocity[axis], axis)
    return grid


def split(value):
    high = value.astype(BF16).astype(F32)
    return high, value - high


def step_kernel(
    n_x, n_y, pop, site_h, frac_h, force_h, count, out,
    site, frac, force, in_v, mom, slots, lhs_hi, lhs_lo, rhs_hi, rhs_lo, acc, rim_r, out_v,
    face_p, face_m, got_p, got_m, side_p, side_m, cor,
    own_sem, in_sem, mark_s, mark_r, face_sem, side_sem, cor_s, cor_r, out_sem,
):
    me_x, me_y = lax.axis_index("gx"), lax.axis_index("gy")
    tiles = in_v.shape[0]
    tile_y = 2 * tiles
    own = site.shape[1]
    right, left = lax.rem(me_x + 1, n_x), lax.rem(me_x + n_x - 1, n_x)
    above, below = lax.rem(me_y + 1, n_y), lax.rem(me_y + n_y - 1, n_y)

    def in_copy(t):
        lanes = pl.ds(pl.multiple_of(t * LANES, LANES), LANES)
        return pltpu.make_async_copy(pop.at[:, :, lanes], in_v.at[t], in_sem.at[t])

    fetches = [
        pltpu.make_async_copy(src, dst, own_sem.at[at])
        for at, (src, dst) in enumerate(((site_h, site), (frac_h, frac), (force_h, force)))
    ]
    for copy in fetches:
        copy.start()

    barrier = pltpu.get_barrier_semaphore()
    near = [(me_x, lax.rem(me_y + k, n_y)) for k in range(1, n_y)]
    near += [(a, lax.rem(me_y + k, n_y)) for a in (right, left) for k in range(n_y)]
    for device in near:
        pl.semaphore_signal(barrier, inc=1, device_id=device, device_id_type=MESH)

    @pl.loop(0, tiles)
    def _(t):
        in_copy(t).start()

    for copy in fetches:
        copy.wait()
    rank = me_y * own + lax.broadcasted_iota(jnp.int32, (3, own), 1)
    slots[0, 0:4, :] = site[...].astype(F32)
    slots[0, 4:7, :] = frac[...]
    slots[0, 7:10, :] = jnp.where(rank < count[0], force[...], 0.0)

    pl.semaphore_wait(barrier, len(near))

    def mark_copy(k):
        return pltpu.make_async_remote_copy(
            src_ref=slots.at[0],
            dst_ref=slots.at[k],
            send_sem=mark_s.at[k],
            recv_sem=mark_r.at[k],
            device_id=(me_x if k < n_y else right, lax.rem(me_y + k, n_y)),
            device_id_type=MESH,
        )

    for k in range(1, 2 * n_y):
        mark_copy(k).start()

    def slot_wait(k):
        pltpu.make_async_remote_copy(
            src_ref=slots.at[0], dst_ref=slots.at[k], send_sem=mark_s.at[k], recv_sem=mark_r.at[k],
            device_id=(left, me_y), device_id_type=MESH,
        ).wait_recv()

    def spread(k, own_column):
        def row(at):
            return jnp.broadcast_to(slots[k, at : at + 1, :], (8, own))

        cells = lax.broadcasted_iota(jnp.int32, (8, own), 0).astype(F32)
        at_y = row(0) * float(tile_y) + row(2) - (me_y * tile_y).astype(F32)
        at_y = jnp.where(at_y < 0.0, at_y + float(tile_y * n_y), at_y)
        next_y = at_y + 1.0
        next_y = jnp.where(next_y == float(tile_y * n_y), 0.0, next_y)
        at_x, at_z = row(1), row(3)
        next_z = jnp.where(at_z == NZ - 1.0, 0.0, at_z + 1.0)
        frac_x, frac_y, frac_z = row(4), row(5), row(6)
        weight_x = jnp.where(
            cells == at_x, 1.0 - frac_x, jnp.where(cells == at_x + 1.0, frac_x, 0.0)
        )
        first = split(weight_x * (1.0 - frac_y))
        second = split(weight_x * frac_y)
        refs = (lhs_hi, lhs_lo)
        for pair in range(tile_y // 2 if own_column else 0):
            picked = [[], []]
            for y in (2 * pair, 2 * pair + 1):
                hit, hit_next = at_y == float(y), next_y == float(y)
                for part in range(2):
                    picked[part].append(
                        jnp.where(hit, first[part], jnp.where(hit_next, second[part], 0.0))
                    )
            for part in range(2):
                refs[part][16 * pair : 16 * pair + 16, :] = jnp.concatenate(picked[part], 0).astype(BF16)
        rim = jnp.where(at_x == 7.0, frac_x, 0.0)
        first = split(rim * (1.0 - frac_y))
        second = split(rim * frac_y)
        for pair in range(0 if own_column else tile_y // 16):
            picked = [[], []]
            for half in range(2):
                rows = cells + float(16 * pair + 8 * half)
                hit, hit_next = at_y == rows, next_y == rows
                for part in range(2):
                    picked[part].append(
                        jnp.where(hit, first[part], jnp.where(hit_next, second[part], 0.0))
                    )
            base = 16 * pair
            for part in range(2):
                refs[part][base : base + 16, :] = jnp.concatenate(picked[part], 0).astype(BF16)
        refs = (rhs_hi, rhs_lo)
        for axis in range(3):
            amount = row(7 + axis)
            first = split(amount * (1.0 - frac_z))
            second = split(amount * frac_z)
            for pair in range(NZ // 16):
                picked = [[], []]
                for half in range(2):
                    rows = cells + float(16 * pair + 8 * half)
                    hit, hit_next = at_z == rows, next_z == rows
                    for part in range(2):
                        picked[part].append(
                            jnp.where(hit, first[part], jnp.where(hit_next, second[part], 0.0))
                        )
                base = axis * NZ + 16 * pair
                for part in range(2):
                    refs[part][base : base + 16, :] = jnp.concatenate(picked[part], 0).astype(BF16)

        def product(a, b):
            return lax.dot_general(
                a[0 : 8 * tile_y if own_column else tile_y, :], b[...], (((1,), (1,)), ((), ())), preferred_element_type=F32
            )

        return product(lhs_hi, rhs_hi) + product(lhs_hi, rhs_lo) + product(lhs_lo, rhs_hi)

    width = 3 * NZ
    main = 8 * tile_y
    acc[0:main, 0:width] = spread(0, True)

    @pl.loop(0, tiles)
    def _(t):
        in_copy(t).wait()
        for at, value in enumerate(raw_moments(lambda q: in_v[t, q])):
            mom[t, at] = value

    @pl.loop(1, n_y)
    def _(k):
        slot_wait(k)
        acc[0:main, 0:width] += spread(k, True)

    rim_r[...] = jnp.zeros_like(rim_r)

    @pl.loop(n_y, 2 * n_y)
    def _(k):
        slot_wait(k)
        rim_r[:, 0:width] += spread(k, False)

    for y in range(tile_y):
        acc[8 * y : 8 * y + 1, :] += rim_r[y : y + 1, :]

    lane = lax.broadcasted_iota(jnp.int32, (8, LANES), 1)
    lower_half = lane < NZ
    z_low = (lane == 0) | (lane == NZ)
    z_high = (lane == NZ - 1) | (lane == LANES - 1)

    def tile_step(t):
        even = acc[pl.ds(pl.multiple_of(16 * t, 16), 8), :]
        odd = acc[pl.ds(pl.multiple_of(16 * t + 8, 8), 8), :]
        a0, a1, b0, b1 = even[:, :LANES], even[:, LANES:], odd[:, :LANES], odd[:, LANES:]
        forces = (
            jnp.where(lower_half, a0, pltpu.roll(b0, NZ, 1)),
            jnp.where(lower_half, pltpu.roll(a0, NZ, 1), b0),
            jnp.where(lower_half, a1, pltpu.roll(b1, NZ, 1)),
        )
        post = collided([mom[t, at] for at in range(10)], forces)
        for i in range(3):
            for j in range(3):
                for k in range(3):
                    q = 9 * i + 3 * j + k
                    value = post[i, j, k]
                    if k == 1:
                        if j != 1:
                            value = pltpu.roll(value, NZ, 1)
                    else:
                        near_by, edge, far = (1, z_low, NZ + 1) if k == 2 else (LANES - 1, z_high, NZ - 1)
                        plain, wrapped = pltpu.roll(value, near_by, 1), pltpu.roll(value, far, 1)
                        if j != 1:
                            plain, wrapped = wrapped, plain
                        value = jnp.where(edge, wrapped, plain)
                    moved = value
                    if i == 2:
                        moved = pltpu.roll(value, 1, 0)
                    elif i == 0:
                        moved = pltpu.roll(value, 7, 0)
                    line = moved if i == 2 else value
                    face = (face_m, None, face_p)[i]
                    at = 3 * j + k
                    if j == 1:
                        out_v[q, t + 1] = moved
                        if i != 1:
                            face[t + 1, at : at + 1, :] = line[0:1, :]
                    else:
                        low_at, high_at = (t + 2, t + 1) if j == 2 else (t + 1, t)
                        out_v[q, low_at, :, 0:NZ] = moved[:, 0:NZ]
                        out_v[q, high_at, :, NZ:] = moved[:, NZ:]
                        if i != 1:
                            face[low_at, at : at + 1, 0:NZ] = line[0:1, 0:NZ]
                            face[high_at, at : at + 1, NZ:] = line[0:1, NZ:]

    def send(src, dst, sems, device):
        return pltpu.make_async_remote_copy(
            src_ref=src, dst_ref=dst, send_sem=sems[0], recv_sem=sems[1],
            device_id=device, device_id_type=MESH,
        )

    corners = []
    for at, (buffer, tile, device) in enumerate(
        (
            (face_p, tiles + 1, (right, above)),
            (face_p, 0, (right, below)),
            (face_m, tiles + 1, (left, above)),
            (face_m, 0, (left, below)),
        )
    ):
        corners.append(send(buffer.at[tile], cor.at[at], (cor_s.at[at], cor_r.at[at]), device))
    sides = []
    for i in range(3):
        sides.append(
            send(out_v.at[pl.ds(9 * i + 6, 3), tiles + 1], side_p.at[pl.ds(3 * i, 3)],
                 (side_sem.at[0, i], side_sem.at[1, i]), (me_x, above))
        )
        sides.append(
            send(out_v.at[pl.ds(9 * i, 3), 0], side_m.at[pl.ds(3 * i, 3)],
                 (side_sem.at[2, i], side_sem.at[3, i]), (me_x, below))
        )
    @pl.loop(0, 2)
    def _(end):
        tile_step(end * (tiles - 1))

    for copy in corners + sides:
        copy.start()

    faces = []
    begin, source = 1, 1
    for part in range(3):
        stop = 1 + (part + 1) * (tiles - 2) // 3

        @pl.loop(begin, stop)
        def _(t):
            tile_step(t)

        end = tiles + 1 if part == 2 else stop
        rows, places = pl.ds(source, end - source), pl.ds(source - 1, end - source)
        for at, (buffer, got, device) in enumerate(
            ((face_p, got_p, (right, me_y)), (face_m, got_m, (left, me_y)))
        ):
            sems = (face_sem.at[2 * at, part], face_sem.at[2 * at + 1, part])
            faces.append(send(buffer.at[rows], got.at[places], sems, device))
        faces[-2].start()
        faces[-1].start()
        begin, source = stop, end

    for copy in sides:
        copy.wait_recv()
    for i in range(3):
        for k in range(3):
            out_v[9 * i + 6 + k, 1, :, 0:NZ] = side_p[3 * i + k, :, 0:NZ]
            out_v[9 * i + k, tiles, :, NZ:] = side_m[3 * i + k, :, NZ:]

    def out_copy(t, group):
        lanes = pl.ds(pl.multiple_of(t * LANES, LANES), LANES)
        rows = pl.ds(9 * group, 9)
        return pltpu.make_async_copy(
            out_v.at[rows, t + 1], out.at[rows, :, lanes], out_sem.at[group, t]
        )

    @pl.loop(0, tiles)
    def _(t):
        for group in range(3):
            out_copy(t, group).start()

    @pl.loop(0, tiles)
    def _(t):
        for group in range(3):
            out_copy(t, group).wait()

    for copy in corners:
        copy.wait_recv()
    for copy in faces:
        copy.wait_recv()
    for k in range(3):
        got_p[0, 6 + k : 7 + k, 0:NZ] = cor[0, 6 + k : 7 + k, 0:NZ]
        got_p[tiles - 1, k : k + 1, NZ:] = cor[1, k : k + 1, NZ:]
        got_m[0, 6 + k : 7 + k, 0:NZ] = cor[2, 6 + k : 7 + k, 0:NZ]
        got_m[tiles - 1, k : k + 1, NZ:] = cor[3, k : k + 1, NZ:]

    @pl.loop(0, tiles)
    def _(t):
        lanes = pl.ds(pl.multiple_of(t * LANES, LANES), LANES)
        for at in range(9):
            out[18 + at, 0:1, lanes] = got_p[t, at : at + 1, :]
            out[at, 7:8, lanes] = got_m[t, at : at + 1, :]

    for k in range(1, 2 * n_y):
        mark_copy(k).wait_send()
    for copy in faces + corners + sides:
        copy.wait_send()


def per_device(n_x, n_y, populations, marker_site, marker_frac, marker_force, marker_count):
    tiles = populations.shape[2] // LANES
    own = marker_site.shape[1]
    tile_y = 2 * tiles
    rows = 8 * tile_y
    width = 3 * NZ
    dma = pltpu.SemaphoreType.DMA
    hbm = pl.BlockSpec(memory_space=pltpu.HBM)
    return pl.pallas_call(
        functools.partial(step_kernel, n_x, n_y),
        out_shape=jax.ShapeDtypeStruct(populations.shape, F32),
        in_specs=[hbm, hbm, hbm, hbm, pl.BlockSpec(memory_space=pltpu.SMEM)],
        out_specs=pl.BlockSpec(memory_space=pltpu.VMEM),
        scratch_shapes=[
            pltpu.VMEM((4, own), jnp.int32),
            pltpu.VMEM((3, own), F32),
            pltpu.VMEM((3, own), F32),
            pltpu.VMEM((tiles, 27, 8, LANES), F32),
            pltpu.VMEM((tiles, 10, 8, LANES), F32),
            pltpu.VMEM((2 * n_y, 10, own), F32),
            pltpu.VMEM((rows, own), BF16),
            pltpu.VMEM((rows, own), BF16),
            pltpu.VMEM((width, own), BF16),
            pltpu.VMEM((width, own), BF16),
            pltpu.VMEM((rows, 2 * LANES), F32),
            pltpu.VMEM((tile_y, 2 * LANES), F32),
            pltpu.VMEM((27, tiles + 2, 8, LANES), F32),
            pltpu.VMEM((tiles + 2, 9, LANES), F32),
            pltpu.VMEM((tiles + 2, 9, LANES), F32),
            pltpu.VMEM((tiles, 9, LANES), F32),
            pltpu.VMEM((tiles, 9, LANES), F32),
            pltpu.VMEM((9, 8, LANES), F32),
            pltpu.VMEM((9, 8, LANES), F32),
            pltpu.VMEM((4, 9, LANES), F32),
            dma((3,)),
            dma((tiles,)),
            dma((2 * n_y,)),
            dma((2 * n_y,)),
            dma((4, 3)),
            dma((4, 3)),
            dma((4,)),
            dma((4,)),
            dma((3, tiles)),
        ],
        compiler_params=pltpu.CompilerParams(
            collective_id=0, has_side_effects=True, vmem_limit_bytes=40 * 1024 * 1024
        ),
    )(*[pltpu.with_memory_space_constraint(value, pltpu.HBM) for value in (populations, marker_site, marker_frac, marker_force)], marker_count)


def solution(mesh):
    in_specs = (
        P(None, "gx", "gy"),
        P(None, ("gx", "gy")),
        P(None, ("gx", "gy")),
        P(None, ("gx", "gy")),
        P("gx"),
    )
    return jax.shard_map(
        functools.partial(per_device, mesh.shape["gx"], mesh.shape["gy"]),
        mesh=mesh,
        in_specs=in_specs,
        out_specs=P(None, "gx", "gy"),
        check_vma=False,
    )
```
